1024 devices in a mesh: row: 32 (over z, y_lo), col: 16 (over y_hi, x), feat: 2 (over core).
Axes of the slice: x: 4, y: 8 (y_hi: 4, y_lo: 2; y = y_hi * 2 + y_lo), z: 16, core: 2. Of those that a mesh axis runs over, the one named last changes fastest.
Arguments:
- features: bfloat16 [262144, 256], P(('row', 'col'), 'feat'), may hold values from -6 to 6
- adj: bfloat16 [2048, 8, 128, 128], P(('row', 'col')), as said below
- col_index: int32 [2048, 8], P(('row', 'col')), may hold values from 0 to 2047, as said below
- weight: bfloat16 [256, 256], replicated, may hold values from -0.375 to 0.375
- centroid: bfloat16 [1024, 256], P(None, 'feat'), may hold values from -5 to 5
- labels: int32 [262144], P(('row', 'col')), may hold values from 0 to 1023
Outputs:
- weight_grad: float32 [256, 256], P('feat')
- feature_grad: bfloat16 [262144, 256], P(('row', 'col'), 'feat')
The draws below stay inside these ranges and needn't reach their ends.
Inputs may be any that keep to these rules, and one draw needn't show every extreme that they name: `col_index`: every column index of block row i lies in its aligned group of 64 block rows, from i - i % 64 to i - i % 64 + 63; indices may repeat within a block row. `adj`: A is symmetric: the blocks of all rows pair one to one so that block s of block row i, at column j = col_index[i, s], is the transpose of a block of block row j at column i.
All inputs are finite; a program needn't handle non-finite values.
Results may differ from the reference program's by a relative error of at most 0.0057.
Values may be sent and summed in bfloat16 or wider, within the bound.
No kernel may reach another device: no remote copies, remote signals or barrier semaphores. Data moves between devices by JAX's collectives and lax.ppermute only.
A program may use at most 32 MiB of HBM per device.

```python
import math
import jax
import jax.numpy as jnp
from jax import lax

BLOCK = 128
NNZ_ROW = 8
FIN = 256
FOUT = 256
CLUSTERS = 1024
GROUP_BLOCKS = 64
BLOCKS_ALL = 2048
NODES = 262144
N_ROW = 32


def neighbour_tables(key):
    base = jax.random.fold_in(key, 11)
    half_count = NNZ_ROW // 2
    keys = jax.random.split(base, N_ROW * half_count)
    forward = jax.vmap(lambda one_key: jax.random.permutation(one_key, GROUP_BLOCKS))(keys).astype(jnp.int32)
    ranks = jnp.arange(GROUP_BLOCKS, dtype=jnp.int32)
    backward = jax.vmap(lambda perm: jnp.zeros_like(perm).at[perm].set(ranks))(forward)
    forward = forward.reshape(N_ROW, half_count, GROUP_BLOCKS)
    backward = backward.reshape(N_ROW, half_count, GROUP_BLOCKS)
    return (forward, backward)


def draw_col_index(key, part):
    forward, backward = neighbour_tables(key)
    local_cols = jnp.concatenate([forward, backward], axis=1)
    local_cols = jnp.transpose(local_cols, (0, 2, 1))
    offsets = jnp.arange(N_ROW, dtype=jnp.int32)[:, None, None] * GROUP_BLOCKS
    return (local_cols + offsets).reshape(BLOCKS_ALL, NNZ_ROW).astype(jnp.int32)


def draw_adj(key, part):
    forward, backward = neighbour_tables(key)
    half_count = NNZ_ROW // 2
    scale = (NNZ_ROW * BLOCK) ** (-0.5)
    shape = (N_ROW, half_count, GROUP_BLOCKS, BLOCK, BLOCK)
    value_key = jax.random.fold_in(key, 23)
    values = jax.random.normal(value_key, shape, jnp.float32) * scale
    partner = jnp.take_along_axis(values, backward[:, :, :, None, None], axis=2)
    partner = jnp.swapaxes(partner, 3, 4)
    joined = jnp.concatenate([values, partner], axis=1)
    joined = jnp.transpose(joined, (0, 2, 1, 3, 4))
    return joined.reshape(BLOCKS_ALL, NNZ_ROW, BLOCK, BLOCK).astype(jnp.bfloat16)


def plant(entries, own_key, low, largest):
    shape = entries.shape
    place = [jax.random.randint(jax.random.fold_in(own_key, axis), (), 0, shape[axis]) for axis in range(len(shape))]
    entries = entries.at[tuple(place)].set(low)
    longest = shape.index(max(shape))
    place[longest] = (place[longest] + 1) % shape[longest]
    return entries.at[tuple(place)].set(largest)


def shard_levels(stream_key, shape, cuts, low, top_value):
    level = 1.0
    for position, blocks in cuts:
        steps = jax.random.uniform(jax.random.fold_in(jax.random.fold_in(stream_key, 6), position), (blocks,), jnp.float32, low / len(cuts), top_value / len(cuts))
        level = level * jnp.repeat(jnp.exp(steps), shape[position] // blocks).reshape((-1,) + (1,) * (len(shape) - 1 - position))
    return level


def bell_draw(rng, dims, spread, reach, pieces=(), kind=jnp.bfloat16):
    entries = jax.random.normal(rng, dims, jnp.float32) * spread
    if len(pieces) > 0:
        entries = shard_levels(rng, dims, pieces, -0.22, 0.18) * entries
    return jnp.clip(entries, min=-reach, max=reach).astype(kind)


def setup_inputs(seed: int = 0) -> dict:
    key_list = jax.random.split(jax.random.key(seed), 7)
    return {
        "features": bell_draw(key_list[0], (NODES, FIN), 1.0, 6.0, ((0, 512), (1, 2))),
        "adj": draw_adj(jax.random.fold_in(key_list[6], 71), 0),
        "col_index": draw_col_index(jax.random.fold_in(key_list[6], 71), 0),
        "weight": bell_draw(key_list[3], (FIN, FOUT), FIN ** -0.5, 0.375),
        "centroid": bell_draw(key_list[4], (CLUSTERS, FOUT), 1.0, 5.0, ((1, 2),)),
        "labels": plant(jax.random.randint(key_list[5], (NODES,), 0, CLUSTERS), jax.random.fold_in(key_list[5], 1), 0, CLUSTERS - 1).astype(jnp.int32),
    }


def silu_slope(value):
    logistic = jax.nn.sigmoid(value)
    return logistic * (1.0 + value * (1.0 - logistic))

def reference(features, adj, col_index, weight, centroid, labels):
    block_count = adj.shape[0]
    nonzero = adj.shape[1]
    block_size = adj.shape[2]
    width_in = features.shape[1]
    node_count = features.shape[0]
    batch = math.gcd(block_count, 64)
    feat_blocks = features.reshape(block_count, block_size, width_in)
    adj_batches = adj.reshape(block_count // batch, batch, nonzero, block_size, block_size)
    col_batches = col_index.reshape(block_count // batch, batch, nonzero)

    def aggregate(pair):
        blocks, columns = pair
        panels = feat_blocks[columns].astype(jnp.float32)
        return jnp.einsum('rkij,rkjf->rif', blocks.astype(jnp.float32), panels, precision=lax.Precision.HIGHEST)
    aggregated = lax.map(aggregate, (adj_batches, col_batches)).reshape(node_count, width_in).astype(jnp.bfloat16)
    logits = jnp.dot(aggregated, weight, preferred_element_type=jnp.float32)
    target = jnp.take(centroid, labels, axis=0).astype(jnp.float32)
    grad_out = ((jax.nn.silu(logits) - target) * silu_slope(logits)).astype(jnp.bfloat16)
    weight_grad = lax.dot_general(aggregated, grad_out, (((0,), (0,)), ((), ())), preferred_element_type=jnp.float32) / math.sqrt(node_count)
    back_projected = lax.dot_general(grad_out, weight, (((1,), (1,)), ((), ())), preferred_element_type=jnp.float32).astype(jnp.bfloat16)
    back_batches = back_projected.reshape(block_count // batch, batch, block_size, width_in)

    def scatter_step(total, triple):
        blocks, columns, back_rows = triple
        contrib = jnp.einsum('rkji,rjf->rkif', blocks.astype(jnp.float32), back_rows.astype(jnp.float32), precision=lax.Precision.HIGHEST)
        total = total.at[columns.reshape(-1)].add(contrib.reshape(-1, block_size, width_in))
        return (total, None)
    start = jnp.zeros((block_count, block_size, width_in), jnp.float32)
    total, _ = lax.scan(scatter_step, start, (adj_batches, col_batches, back_batches))
    feature_grad = total.reshape(node_count, width_in).astype(jnp.bfloat16)
    return (weight_grad, feature_grad)
```

```python
import math

import jax
import jax.numpy as jnp
from jax import lax
from jax.experimental import pallas as pl
from jax.experimental.pallas import tpu as pltpu
from jax.sharding import PartitionSpec as P

SIDE = 4


def product_kernel(offset_ref, adj_ref, *rest):
    parts = rest[:-5]
    out_ref, adj_held, panels, adj_sem, part_sems = rest[-5:]
    block_rows, nonzero, block, _ = adj_held.shape
    adj_copy = pltpu.make_async_copy(adj_ref, adj_held, adj_sem)
    adj_copy.start()
    copies = []
    start = 0
    for index, part in enumerate(parts):
        rows = part.shape[0]
        copy = pltpu.make_async_copy(part, panels.at[pl.ds(start, rows)], part_sems.at[index])
        copy.start()
        copies.append(copy)
        start += rows
    adj_copy.wait()
    for copy in copies:
        copy.wait()
    for r in range(block_rows):
        left = jnp.concatenate([adj_held[r, k] for k in range(nonzero)], axis=1)
        right = jnp.concatenate(
            [panels[pl.ds(pl.multiple_of(offset_ref[r, k], block), block), :] for k in range(nonzero)],
            axis=0,
        )
        total = jnp.dot(left, right, preferred_element_type=jnp.float32)
        out_ref[pl.ds(r * block, block), :] = total.astype(out_ref.dtype)


def block_product(offsets, adj, parts):
    block_rows, nonzero, block, _ = adj.shape
    width = parts[0].shape[1]
    held = sum(part.shape[0] for part in parts)
    return pl.pallas_call(
        product_kernel,
        out_shape=jax.ShapeDtypeStruct((block_rows * block, width), jnp.bfloat16),
        in_specs=[pl.BlockSpec(memory_space=pltpu.SMEM)]
        + [pl.BlockSpec(memory_space=pl.ANY)] * (1 + len(parts)),
        out_specs=pl.BlockSpec(memory_space=pltpu.VMEM),
        scratch_shapes=[
            pltpu.VMEM(adj.shape, adj.dtype),
            pltpu.VMEM((held, width), jnp.bfloat16),
            pltpu.SemaphoreType.DMA,
            pltpu.SemaphoreType.DMA((len(parts),)),
        ],
        cost_estimate=pl.CostEstimate(
            flops=2 * block_rows * nonzero * block * block * width,
            bytes_accessed=2 * (adj.size + held * width),
            transcendentals=0,
        ),
        name="block_product",
    )(offsets, adj, *parts)


def middle_kernel(own_ref, other_ref, weight_ref, mine_ref, theirs_ref, partial_ref, back_ref):
    half = own_ref.shape[1]
    own = own_ref[...]
    logits = jnp.dot(own, weight_ref[:half, :], preferred_element_type=jnp.float32)
    logits += jnp.dot(other_ref[...], weight_ref[half:, :], preferred_element_type=jnp.float32)
    target = jnp.concatenate([mine_ref[...], theirs_ref[...]], axis=1).astype(jnp.float32)
    logistic = jax.nn.sigmoid(logits)
    slope = logistic * (1.0 + logits * (1.0 - logistic))
    grad_out = ((logits * logistic - target) * slope).astype(jnp.bfloat16)
    partial_ref[...] = lax.dot_general(
        own, grad_out, (((0,), (0,)), ((), ())), preferred_element_type=jnp.float32
    )
    back_ref[...] = lax.dot_general(
        grad_out, weight_ref[:half, :], (((1,), (1,)), ((), ())), preferred_element_type=jnp.float32
    ).astype(jnp.bfloat16)


def middle(own, other, weight, mine, theirs):
    rows, half = own.shape
    return pl.pallas_call(
        middle_kernel,
        out_shape=(
            jax.ShapeDtypeStruct((half, weight.shape[1]), jnp.float32),
            jax.ShapeDtypeStruct((rows, half), jnp.bfloat16),
        ),
        cost_estimate=pl.CostEstimate(
            flops=2 * rows * weight.size * 2, bytes_accessed=8 * rows * half, transcendentals=rows * weight.shape[1]
        ),
        name="middle",
    )(own, other, weight, mine, theirs)


def from_col(value, dy, dx):
    pairs = []
    for y in range(SIDE):
        for x in range(SIDE):
            pairs.append((((y + dy) % SIDE) * SIDE + (x + dx) % SIDE, y * SIDE + x))
    return lax.ppermute(value, "col", pairs)


def swap_x(value, bits):
    return lax.ppermute(value, "col", [(c, c ^ bits) for c in range(SIDE * SIDE)])


def gather_group(value):
    rows = value.shape[0]
    far = from_col(value, 2, 0)
    column = jnp.concatenate([value, from_col(value, 1, 0), far, from_col(value, 3, 0)], axis=0)
    right = from_col(column, 0, 1)
    left = from_col(column, 0, 3)
    low = from_col(right[: 2 * rows], 0, 1)
    high = from_col(left[2 * rows :], 0, 3)
    return [column, right, low, high, left]


def sum_weight(partial, row_size):
    x = lax.axis_index("col") % SIDE
    first = (x ^ (x >> 1)) & 1
    second = x >> 1
    for bits, bit in ((1, first), (3, second)):
        rows = partial.shape[0] // 2
        kept = lax.dynamic_slice_in_dim(partial, bit * rows, rows, 0)
        sent = lax.dynamic_slice_in_dim(partial, (1 - bit) * rows, rows, 0)
        partial = kept + swap_x(sent, bits)
    for bits in (SIDE, 3 * SIDE):
        partial = partial + swap_x(partial, bits)
    step = 1
    while step < row_size:
        partial = partial + lax.ppermute(partial, "row", [(r, r ^ step) for r in range(row_size)])
        step *= 2
    for bits, bit in ((3, second), (1, first)):
        other = swap_x(partial, bits)
        partial = jnp.where(
            bit == 0,
            jnp.concatenate([partial, other], axis=0),
            jnp.concatenate([other, partial], axis=0),
        )
    return partial


def per_device(features, adj, col_index, weight, centroid, labels):
    block_rows, nonzero, block, _ = adj.shape
    row_count, half = features.shape
    feat = lax.axis_index("feat")
    col = lax.axis_index("col")
    row_size, col_size = lax.axis_size("row"), lax.axis_size("col")
    node_count = row_count * row_size * col_size
    local = col_index % (block_rows * col_size)
    owner = local // block_rows
    down = (owner // SIDE - col // SIDE) % SIDE
    along = (owner % SIDE - col % SIDE) % SIDE
    offsets = ((along * SIDE + down) * block_rows + local % block_rows) * block

    parts = gather_group(features)
    label_table = (
        labels[:, None] == jnp.arange(centroid.shape[0], dtype=jnp.int32)[None, :]
    ).astype(jnp.bfloat16)
    mine = jnp.dot(label_table, centroid, preferred_element_type=jnp.float32).astype(jnp.bfloat16)
    theirs = lax.ppermute(mine, "feat", [(0, 1), (1, 0)])
    swapped = jnp.roll(weight, (half, centroid.shape[1]), (0, 1))
    turned = jnp.where(feat == 0, weight, swapped)

    own = block_product(offsets, adj, parts)
    other = lax.ppermute(own, "feat", [(0, 1), (1, 0)])
    partial, back = middle(own, other, turned, mine, theirs)
    feature_grad = block_product(offsets, adj, gather_group(back))
    total = sum_weight(partial, row_size) * (1.0 / math.sqrt(node_count))
    weight_grad = jnp.where(feat == 0, total, jnp.roll(total, half, 1))
    return (weight_grad, feature_grad)


def solution(mesh):
    placed = (
        P(("row", "col"), "feat"),
        P(("row", "col"), None, None, None),
        P(("row", "col"), None),
        P(),
        P(None, "feat"),
        P(("row", "col")),
    )
    return jax.shard_map(
        per_device,
        mesh=mesh,
        in_specs=placed,
        out_specs=(P("feat", None), P(("row", "col"), "feat")),
        check_vma=False,
    )
```

```python
import math

import jax
import jax.numpy as jnp
from jax import lax
from jax.experimental import pallas as pl
from jax.experimental.pallas import tpu as pltpu
from jax.sharding import PartitionSpec as P

SIDE = 4


def product_kernel(offset_ref, adj_ref, panel_ref, *rest):
    out_ref, adj_held, held, adj_sems, panel_sems = rest[-5:]
    block_rows, nonzero, block, _ = adj_held.shape

    def fetch(r, k):
        start = pl.multiple_of(offset_ref[r, k], block)
        return pltpu.make_async_copy(
            panel_ref.at[pl.ds(start, block)], held.at[r, pl.ds(k * block, block)], panel_sems.at[r, k]
        )

    adj_copies = []
    for r in range(block_rows):
        copy = pltpu.make_async_copy(adj_ref.at[r], adj_held.at[r], adj_sems.at[r])
        copy.start()
        adj_copies.append(copy)
        for k in range(nonzero):
            fetch(r, k).start()
    if len(rest) == 6:
        out_ref[pl.ds(block_rows * block, rest[0].shape[0]), :] = rest[0][...]
    for r in range(block_rows):
        adj_copies[r].wait()
        for k in range(nonzero):
            fetch(r, k).wait()
        left = jnp.concatenate([adj_held[r, k] for k in range(nonzero)], axis=1)
        total = jnp.dot(left, held[r], preferred_element_type=jnp.float32)
        out_ref[pl.ds(r * block, block), :] = total.astype(out_ref.dtype)


def block_product(offsets, adj, panels, carried=(), place=pl.ANY):
    block_rows, nonzero, block, _ = adj.shape
    width = panels.shape[1]
    rows = block_rows * block + sum(array.shape[0] for array in carried)
    return pl.pallas_call(
        product_kernel,
        out_shape=jax.ShapeDtypeStruct((rows, width), jnp.bfloat16),
        in_specs=[
            pl.BlockSpec(memory_space=pltpu.SMEM),
            pl.BlockSpec(memory_space=pl.ANY),
            pl.BlockSpec(memory_space=place),
        ]
        + [pl.BlockSpec(memory_space=pltpu.VMEM)] * len(carried),
        out_specs=pl.BlockSpec(memory_space=pltpu.VMEM),
        scratch_shapes=[
            pltpu.VMEM(adj.shape, adj.dtype),
            pltpu.VMEM((block_rows, nonzero * block, width), jnp.bfloat16),
            pltpu.SemaphoreType.DMA((block_rows,)),
            pltpu.SemaphoreType.DMA((block_rows, nonzero)),
        ],
        compiler_params=pltpu.CompilerParams(vmem_limit_bytes=12 << 20),
        cost_estimate=pl.CostEstimate(
            flops=2 * block_rows * nonzero * block * block * width,
            bytes_accessed=2 * (adj.size + block_rows * nonzero * block * width),
            transcendentals=0,
        ),
        name="block_product",
    )(offsets, adj, panels, *carried)


def middle_kernel(here_ref, there_ref, weight_ref, partial_ref, back_ref):
    rows, half = back_ref.shape
    own = here_ref[:rows, :]
    logits = jnp.dot(own, weight_ref[:half, :], preferred_element_type=jnp.float32)
    logits += jnp.dot(there_ref[:rows, :], weight_ref[half:, :], preferred_element_type=jnp.float32)
    target = jnp.concatenate([here_ref[rows:, :], there_ref[rows:, :]], axis=1).astype(jnp.float32)
    logistic = jax.nn.sigmoid(logits)
    slope = logistic * (1.0 + logits * (1.0 - logistic))
    grad_out = ((logits * logistic - target) * slope).astype(jnp.bfloat16)
    back_ref[...] = lax.dot_general(
        grad_out, weight_ref[:half, :], (((1,), (1,)), ((), ())), preferred_element_type=jnp.float32
    ).astype(jnp.bfloat16)
    partial_ref[...] = lax.dot_general(
        own, grad_out, (((0,), (0,)), ((), ())), preferred_element_type=jnp.float32
    )


def middle(here, there, weight):
    rows, half = here.shape[0] // 2, here.shape[1]
    return pl.pallas_call(
        middle_kernel,
        out_shape=(
            jax.ShapeDtypeStruct((half, weight.shape[1]), jnp.float32),
            jax.ShapeDtypeStruct((rows, half), jnp.bfloat16),
        ),
        compiler_params=pltpu.CompilerParams(vmem_limit_bytes=12 << 20),
        cost_estimate=pl.CostEstimate(
            flops=4 * rows * weight.size, bytes_accessed=12 * rows * half, transcendentals=rows * weight.shape[1]
        ),
        name="middle",
    )(here, there, weight)


def to_all(value, axis, count, groups=None):
    copies = jnp.broadcast_to(value[None], (count, *value.shape))
    return lax.all_to_all(copies, axis, 0, 0, axis_index_groups=groups)


def gather_group(value):
    along_y = [[y * SIDE + x for y in range(SIDE)] for x in range(SIDE)]
    along_x = [[y * SIDE + x for x in range(SIDE)] for y in range(SIDE)]
    column = to_all(value, "col", SIDE, along_y).reshape(-1, value.shape[1])
    return to_all(column, "col", SIDE, along_x).reshape(-1, value.shape[1])


def sum_weight(partial, row_size, col_size):
    rows, width = partial.shape
    pieces = lax.all_to_all(partial.reshape(col_size, rows // col_size, width), "col", 0, 0)
    piece = to_all(pieces.sum(0), "row", row_size).sum(0)
    return to_all(piece, "col", col_size).reshape(rows, width)


def per_device(features, adj, col_index, weight, centroid, labels):
    block_rows, nonzero, block, _ = adj.shape
    row_count, half = features.shape
    feat = lax.axis_index("feat")
    row_size, col_size = lax.axis_size("row"), lax.axis_size("col")
    node_count = row_count * row_size * col_size
    local = col_index % (block_rows * col_size)
    owner = local // block_rows
    turned_offsets = (((owner % SIDE) * SIDE + owner // SIDE) * block_rows + local % block_rows) * block

    label_table = (
        labels[:, None] == jnp.arange(centroid.shape[0], dtype=jnp.int32)[None, :]
    ).astype(jnp.bfloat16)
    target = jnp.dot(label_table, centroid, preferred_element_type=jnp.float32).astype(jnp.bfloat16)
    swapped = jnp.roll(weight, (half, centroid.shape[1]), (0, 1))
    turned = jnp.where(feat == 0, weight, swapped)

    here = block_product(turned_offsets, adj, gather_group(features), (target,))
    there = lax.ppermute(here, "feat", [(0, 1), (1, 0)])
    partial, back = middle(here, there, turned)
    gathered = lax.all_gather(back, "col", axis=0, tiled=True)
    feature_grad = block_product(local * block, adj, gathered, place=pltpu.HBM)
    total = sum_weight(partial, row_size, col_size) * (1.0 / math.sqrt(node_count))
    weight_grad = jnp.where(feat == 0, total, jnp.roll(total, half, 1))
    return (weight_grad, feature_grad)


def solution(mesh):
    placed = (
        P(("row", "col"), "feat"),
        P(("row", "col"), None, None, None),
        P(("row", "col"), None),
        P(),
        P(None, "feat"),
        P(("row", "col")),
    )
    return jax.shard_map(
        per_device,
        mesh=mesh,
        in_specs=placed,
        out_specs=(P("feat", None), P(("row", "col"), "feat")),
        check_vma=False,
    )
```

```python
import functools
import math

import jax
import jax.numpy as jnp
from jax import lax
from jax.experimental import pallas as pl
from jax.experimental.pallas import tpu as pltpu
from jax.sharding import PartitionSpec as P

SIDE = 4
Y_LO = 2


def product_kernel(count, which_ref, offset_ref, adj_ref, *rest):
    parts, carried = rest[:count], rest[count:-2]
    out_ref, held = rest[-2:]
    block_rows, nonzero, block, _ = adj_ref.shape

    def place(part, r, k, start):
        held[r, pl.ds(k * block, block), :] = part[pl.ds(start, block), :]

    for r in range(block_rows):
        for k in range(nonzero):
            start = pl.multiple_of(offset_ref[r, k], block)
            if count == 1:
                place(parts[0], r, k, start)
            else:
                for index, part in enumerate(parts):
                    pl.when(which_ref[r, k] == index)(functools.partial(place, part, r, k, start))
    for array in carried:
        out_ref[pl.ds(block_rows * block, array.shape[0]), :] = array[...]
    for r in range(block_rows):
        left = jnp.concatenate([adj_ref[r, k] for k in range(nonzero)], axis=1)
        total = jnp.dot(left, held[r], preferred_element_type=jnp.float32)
        out_ref[pl.ds(r * block, block), :] = total.astype(out_ref.dtype)


def block_product(which, offsets, adj, parts, carried=()):
    block_rows, nonzero, block, _ = adj.shape
    width = parts[0].shape[1]
    rows = block_rows * block + sum(array.shape[0] for array in carried)
    whole = pl.BlockSpec(memory_space=pltpu.VMEM)
    return pl.pallas_call(
        functools.partial(product_kernel, len(parts)),
        out_shape=jax.ShapeDtypeStruct((rows, width), jnp.bfloat16),
        in_specs=[pl.BlockSpec(memory_space=pltpu.SMEM)] * 2 + [whole] * (1 + len(parts) + len(carried)),
        out_specs=whole,
        scratch_shapes=[pltpu.VMEM((block_rows, nonzero * block, width), jnp.bfloat16)],
        compiler_params=pltpu.CompilerParams(vmem_limit_bytes=14 << 20),
        cost_estimate=pl.CostEstimate(
            flops=2 * block_rows * nonzero * block * block * width,
            bytes_accessed=2 * (adj.size + block_rows * nonzero * block * width),
            transcendentals=0,
        ),
        name="block_product",
    )(which, offsets, adj, *parts, *carried)


def middle_kernel(here_ref, there_ref, weight_ref, parcel_ref):
    half = here_ref.shape[1]
    rows = here_ref.shape[0] // 2
    own = here_ref[:rows, :]
    logits = jnp.dot(own, weight_ref[:half, :], preferred_element_type=jnp.float32)
    logits += jnp.dot(there_ref[:rows, :], weight_ref[half:, :], preferred_element_type=jnp.float32)
    target = jnp.concatenate([here_ref[rows:, :], there_ref[rows:, :]], axis=1).astype(jnp.float32)
    logistic = jax.nn.sigmoid(logits)
    slope = logistic * (1.0 + logits * (1.0 - logistic))
    grad_out = ((logits * logistic - target) * slope).astype(jnp.bfloat16)
    back = lax.dot_general(
        grad_out, weight_ref[:half, :], (((1,), (1,)), ((), ())), preferred_element_type=jnp.float32
    ).astype(jnp.bfloat16)
    partial = lax.dot_general(own, grad_out, (((0,), (0,)), ((), ())), preferred_element_type=jnp.float32)
    head = partial.astype(jnp.bfloat16)
    rest = (partial - head.astype(jnp.float32)).astype(jnp.bfloat16)
    count = parcel_ref.shape[0]
    quarter = half // count
    width = partial.shape[1]
    for y in range(count):
        parcel_ref[y, :rows, :] = back
        start = rows
        for values in (head, rest):
            for first in range(0, width, half):
                parcel_ref[y, start : start + quarter, :] = values[y * quarter : (y + 1) * quarter, first : first + half]
                start += quarter


def middle(here, there, weight):
    rows, half = here.shape[0] // 2, here.shape[1]
    extra = 2 * weight.shape[1] // SIDE
    return pl.pallas_call(
        middle_kernel,
        out_shape=jax.ShapeDtypeStruct((SIDE, rows + extra, half), jnp.bfloat16),
        compiler_params=pltpu.CompilerParams(vmem_limit_bytes=14 << 20),
        cost_estimate=pl.CostEstimate(
            flops=4 * rows * weight.size, bytes_accessed=12 * rows * half, transcendentals=rows * weight.shape[1]
        ),
        name="middle",
    )(here, there, weight)


WHOLE = pl.BlockSpec(memory_space=pltpu.VMEM)
SMALL = pltpu.CompilerParams(vmem_limit_bytes=4 << 20)


def open_kernel(skip, parcels_ref, out_ref):
    count, rows, _ = parcels_ref.shape
    pieces = parcels_ref[:, skip:, :].astype(jnp.float32)
    both = pieces[:, : (rows - skip) // 2, :] + pieces[:, (rows - skip) // 2 :, :]
    out_ref[...] = both.sum(0)


def open_parcels(parcels, skip):
    return pl.pallas_call(
        functools.partial(open_kernel, skip),
        out_shape=jax.ShapeDtypeStruct(((parcels.shape[1] - skip) // 2, parcels.shape[2]), jnp.float32),
        in_specs=[WHOLE],
        out_specs=WHOLE,
        compiler_params=SMALL,
        name="open_parcels",
    )(parcels)


def spread_kernel(pieces_ref, *rest):
    out_ref = rest[-1]
    total = pieces_ref[...].sum(0)
    for index in range(out_ref.shape[0]):
        out_ref[index] = total


def spread_sum(pieces, count, after):
    return pl.pallas_call(
        spread_kernel,
        out_shape=jax.ShapeDtypeStruct((count, *pieces.shape[1:]), pieces.dtype),
        in_specs=[WHOLE] + [pl.BlockSpec(memory_space=pl.ANY)] * len(after),
        out_specs=WHOLE,
        compiler_params=SMALL,
        name="spread_sum",
    )(pieces, *after)


def settle_kernel(scale, feat_ref, pieces_ref, out_ref):
    halves, half = out_ref.shape[1] // pieces_ref.shape[2], pieces_ref.shape[2]
    per_half = pieces_ref.shape[0] // halves
    for index in range(halves):
        values = pieces_ref[pl.ds((index ^ feat_ref[0]) * per_half, per_half)] * scale
        out_ref[:, index * half : (index + 1) * half] = values.reshape(out_ref.shape[0], half)


def settle(feat, pieces, scale):
    count, rows, half = pieces.shape
    return pl.pallas_call(
        functools.partial(settle_kernel, scale),
        out_shape=jax.ShapeDtypeStruct((count * rows // 2, 2 * half), pieces.dtype),
        in_specs=[pl.BlockSpec(memory_space=pltpu.SMEM), WHOLE],
        out_specs=WHOLE,
        compiler_params=SMALL,
        name="settle",
    )(feat.reshape(1), pieces)


def to_all(value, axis, count, groups=None):
    copies = jnp.broadcast_to(value[None], (count, *value.shape))
    return lax.all_to_all(copies, axis, 0, 0, axis_index_groups=groups)


ALONG_Y = [[y * SIDE + x for y in range(SIDE)] for x in range(SIDE)]
ALONG_X = [[y * SIDE + x for x in range(SIDE)] for y in range(SIDE)]


def from_x(value, dx):
    pairs = [(y * SIDE + (x + dx) % SIDE, y * SIDE + x) for y in range(SIDE) for x in range(SIDE)]
    return lax.ppermute(value, "col", pairs)


def sum_weight(quarter, row_size, sides, far):
    both = ("row", "col")
    col_size = SIDE * SIDE
    layers = row_size // Y_LO
    near = Y_LO * col_size
    mates = [
        [(z * Y_LO + lo) * col_size + y * SIDE + x for lo in range(Y_LO) for x in range(SIDE)]
        for z in range(layers)
        for y in range(SIDE)
    ]
    depth = [[z * near + i for z in range(layers)] for i in range(near)]
    plane = [[z * near + i for i in range(near)] for z in range(layers)]
    pieces = quarter.reshape(Y_LO * SIDE, -1, quarter.shape[1])
    pieces = lax.all_to_all(pieces, both, 0, 0, axis_index_groups=mates)
    pieces = lax.all_to_all(spread_sum(pieces, layers, sides), both, 0, 0, axis_index_groups=depth)
    return lax.all_to_all(spread_sum(pieces, near, far), both, 0, 0, axis_index_groups=plane)


def per_device(features, adj, col_index, weight, centroid, labels):
    block_rows, nonzero, block, _ = adj.shape
    row_count, half = features.shape
    feat = lax.axis_index("feat")
    row_size, col_size = lax.axis_size("row"), lax.axis_size("col")
    node_count = row_count * row_size * col_size
    local = col_index % (block_rows * col_size)
    owner = local // block_rows
    owner_y, owner_x = owner // SIDE, owner % SIDE
    within = (local % block_rows) * block

    label_table = (
        labels[:, None] == jnp.arange(centroid.shape[0], dtype=jnp.int32)[None, :]
    ).astype(jnp.bfloat16)
    target = jnp.dot(label_table, centroid, preferred_element_type=jnp.float32).astype(jnp.bfloat16)
    swapped = jnp.roll(weight, (half, centroid.shape[1]), (0, 1))
    turned = jnp.where(feat == 0, weight, swapped)

    column = to_all(features, "col", SIDE, ALONG_Y).reshape(-1, half)
    panels = to_all(column, "col", SIDE, ALONG_X).reshape(-1, half)
    offsets = (owner_x * SIDE + owner_y) * row_count + within
    here = block_product(offsets, offsets, adj, [panels], (target,))
    there = lax.ppermute(here, "feat", [(0, 1), (1, 0)])

    parcels = lax.all_to_all(middle(here, there, turned), "col", 0, 0, axis_index_groups=ALONG_Y)
    stride = parcels.shape[1]
    column = parcels.reshape(-1, half)
    parts = [column] + [from_x(column, dx) for dx in range(1, SIDE)]
    which = (owner_x - lax.axis_index("col")) % SIDE
    feature_grad = block_product(which, owner_y * stride + within, adj, parts)

    sides, far = (parts[1], parts[3]), (parts[2],)
    pieces = sum_weight(open_parcels(parcels, row_count), row_size, sides, far)
    weight_grad = settle(feat, pieces, 1.0 / math.sqrt(node_count))
    return (weight_grad, feature_grad)


def solution(mesh):
    placed = (
        P(("row", "col"), "feat"),
        P(("row", "col"), None, None, None),
        P(("row", "col"), None),
        P(),
        P(None, "feat"),
        P(("row", "col")),
    )
    return jax.shard_map(
        per_device,
        mesh=mesh,
        in_specs=placed,
        out_specs=(P("feat", None), P(("row", "col"), "feat")),
        check_vma=False,
    )
```

```python
import functools
import math

import jax
import jax.numpy as jnp
from jax import lax
from jax.experimental import pallas as pl
from jax.experimental.pallas import tpu as pltpu
from jax.sharding import PartitionSpec as P

SIDE = 4
Y_LO = 2


def product_kernel(count, which_ref, offset_ref, adj_ref, *rest):
    parts, carried = rest[:count], rest[count:-2]
    out_ref, held = rest[-2:]
    block_rows, nonzero, block, _ = adj_ref.shape

    def place(part, r, k, start):
        held[r, pl.ds(k * block, block), :] = part[pl.ds(start, block), :]

    for r in range(block_rows):
        for k in range(nonzero):
            start = pl.multiple_of(offset_ref[r, k], block)
            if count == 1:
                place(parts[0], r, k, start)
            else:
                for index, part in enumerate(parts):
                    pl.when(which_ref[r, k] == index)(functools.partial(place, part, r, k, start))
    for array in carried:
        out_ref[pl.ds(block_rows * block, array.shape[0]), :] = array[...]
    for r in range(block_rows):
        left = jnp.concatenate([adj_ref[r, k] for k in range(nonzero)], axis=1)
        total = jnp.dot(left, held[r], preferred_element_type=jnp.float32)
        out_ref[pl.ds(r * block, block), :] = total.astype(out_ref.dtype)


def block_product(which, offsets, adj, parts, carried=()):
    block_rows, nonzero, block, _ = adj.shape
    width = parts[0].shape[1]
    rows = block_rows * block + sum(array.shape[0] for array in carried)
    whole = pl.BlockSpec(memory_space=pltpu.VMEM)
    return pl.pallas_call(
        functools.partial(product_kernel, len(parts)),
        out_shape=jax.ShapeDtypeStruct((rows, width), jnp.bfloat16),
        in_specs=[pl.BlockSpec(memory_space=pltpu.SMEM)] * 2 + [whole] * (1 + len(parts) + len(carried)),
        out_specs=whole,
        scratch_shapes=[pltpu.VMEM((block_rows, nonzero * block, width), jnp.bfloat16)],
        compiler_params=pltpu.CompilerParams(vmem_limit_bytes=14 << 20),
        cost_estimate=pl.CostEstimate(
            flops=2 * block_rows * nonzero * block * block * width,
            bytes_accessed=2 * (adj.size + block_rows * nonzero * block * width),
            transcendentals=0,
        ),
        name="block_product",
    )(which, offsets, adj, *parts, *carried)


def middle_kernel(here_ref, there_ref, weight_ref, partial_ref, back_ref):
    half = here_ref.shape[1]
    rows = here_ref.shape[0] // 2
    own = here_ref[:rows, :]
    logits = jnp.dot(own, weight_ref[:half, :], preferred_element_type=jnp.float32)
    logits += jnp.dot(there_ref[:rows, :], weight_ref[half:, :], preferred_element_type=jnp.float32)
    target = jnp.concatenate([here_ref[rows:, :], there_ref[rows:, :]], axis=1).astype(jnp.float32)
    logistic = jax.nn.sigmoid(logits)
    slope = logistic * (1.0 + logits * (1.0 - logistic))
    grad_out = ((logits * logistic - target) * slope).astype(jnp.bfloat16)
    back = lax.dot_general(
        grad_out, weight_ref[:half, :], (((1,), (1,)), ((), ())), preferred_element_type=jnp.float32
    ).astype(jnp.bfloat16)
    for y in range(back_ref.shape[0]):
        back_ref[y] = back
    partial = lax.dot_general(own, grad_out, (((0,), (0,)), ((), ())), preferred_element_type=jnp.float32)
    for index in range(partial_ref.shape[0]):
        partial_ref[index] = partial[:, index * half : (index + 1) * half]


def middle(here, there, weight):
    rows, half = here.shape[0] // 2, here.shape[1]
    return pl.pallas_call(
        middle_kernel,
        out_shape=(
            jax.ShapeDtypeStruct((weight.shape[1] // half, half, half), jnp.float32),
            jax.ShapeDtypeStruct((SIDE, rows, half), jnp.bfloat16),
        ),
        compiler_params=pltpu.CompilerParams(vmem_limit_bytes=14 << 20),
        cost_estimate=pl.CostEstimate(
            flops=4 * rows * weight.size, bytes_accessed=12 * rows * half, transcendentals=rows * weight.shape[1]
        ),
        name="middle",
    )(here, there, weight)


WHOLE = pl.BlockSpec(memory_space=pltpu.VMEM)
SMALL = pltpu.CompilerParams(vmem_limit_bytes=4 << 20)


def spread_kernel(pieces_ref, *rest):
    out_ref = rest[-1]
    total = pieces_ref[...].sum(0)
    for index in range(out_ref.shape[0]):
        out_ref[index] = total


def spread_sum(pieces, count, after=()):
    return pl.pallas_call(
        spread_kernel,
        out_shape=jax.ShapeDtypeStruct((count, *pieces.shape[1:]), pieces.dtype),
        in_specs=[WHOLE] + [pl.BlockSpec(memory_space=pl.ANY)] * len(after),
        out_specs=WHOLE,
        compiler_params=SMALL,
        name="spread_sum",
    )(pieces, *after)


def settle_kernel(scale, feat_ref, pieces_ref, out_ref):
    halves, half = out_ref.shape[1] // pieces_ref.shape[2], pieces_ref.shape[2]
    per_half = pieces_ref.shape[0] // halves
    for index in range(halves):
        values = pieces_ref[pl.ds((index ^ feat_ref[0]) * per_half, per_half)] * scale
        out_ref[:, index * half : (index + 1) * half] = values.reshape(out_ref.shape[0], half)


def settle(feat, pieces, scale):
    count, rows, half = pieces.shape
    return pl.pallas_call(
        functools.partial(settle_kernel, scale),
        out_shape=jax.ShapeDtypeStruct((count * rows // 2, 2 * half), pieces.dtype),
        in_specs=[pl.BlockSpec(memory_space=pltpu.SMEM), WHOLE],
        out_specs=WHOLE,
        compiler_params=SMALL,
        name="settle",
    )(feat.reshape(1), pieces)


def to_all(value, axis, count, groups=None):
    copies = jnp.broadcast_to(value[None], (count, *value.shape))
    return lax.all_to_all(copies, axis, 0, 0, axis_index_groups=groups)


ALONG_Y = [[y * SIDE + x for y in range(SIDE)] for x in range(SIDE)]
ALONG_X = [[y * SIDE + x for x in range(SIDE)] for y in range(SIDE)]


def sum_weight(pieces, row_size):
    both = ("row", "col")
    layers = row_size // Y_LO
    near = pieces.shape[0]
    depth = [[z * near + i for z in range(layers)] for i in range(near)]
    plane = [[z * near + i for i in range(near)] for z in range(layers)]
    pieces = lax.all_to_all(pieces, both, 0, 0, axis_index_groups=plane)
    pieces = lax.all_to_all(spread_sum(pieces, layers), both, 0, 0, axis_index_groups=depth)
    return lax.all_to_all(spread_sum(pieces, near), both, 0, 0, axis_index_groups=plane)


def per_device(features, adj, col_index, weight, centroid, labels):
    block_rows, nonzero, block, _ = adj.shape
    row_count, half = features.shape
    feat = lax.axis_index("feat")
    row_size, col_size = lax.axis_size("row"), lax.axis_size("col")
    node_count = row_count * row_size * col_size
    local = col_index % (block_rows * col_size)
    owner = local // block_rows
    owner_y, owner_x = owner // SIDE, owner % SIDE
    within = (local % block_rows) * block

    label_table = (
        labels[:, None] == jnp.arange(centroid.shape[0], dtype=jnp.int32)[None, :]
    ).astype(jnp.bfloat16)
    target = jnp.dot(label_table, centroid, preferred_element_type=jnp.float32).astype(jnp.bfloat16)
    swapped = jnp.roll(weight, (half, centroid.shape[1]), (0, 1))
    turned = jnp.where(feat == 0, weight, swapped)

    column = to_all(features, "col", SIDE, ALONG_Y).reshape(-1, half)
    panels = to_all(column, "col", SIDE, ALONG_X).reshape(-1, half)
    offsets = (owner_x * SIDE + owner_y) * row_count + within
    here = block_product(offsets, offsets, adj, [panels], (target,))
    there = lax.ppermute(here, "feat", [(0, 1), (1, 0)])

    partial, back = middle(here, there, turned)
    column = lax.all_to_all(back, "col", 0, 0, axis_index_groups=ALONG_Y).reshape(-1, half)
    gathered = lax.all_gather(column, "col", axis=0, tiled=True, axis_index_groups=ALONG_X)
    feature_grad = block_product(offsets, offsets, adj, [gathered])

    pieces = sum_weight(partial.reshape(Y_LO * col_size, -1, half), row_size)
    weight_grad = settle(feat, pieces, 1.0 / math.sqrt(node_count))
    return (weight_grad, feature_grad)


def solution(mesh):
    placed = (
        P(("row", "col"), "feat"),
        P(("row", "col"), None, None, None),
        P(("row", "col"), None),
        P(),
        P(None, "feat"),
        P(("row", "col")),
    )
    return jax.shard_map(
        per_device,
        mesh=mesh,
        in_specs=placed,
        out_specs=(P("feat", None), P(("row", "col"), "feat")),
        check_vma=False,
    )
```

```python
import functools
import math

import jax
import jax.numpy as jnp
from jax import lax
from jax.experimental import pallas as pl
from jax.experimental.pallas import tpu as pltpu
from jax.sharding import PartitionSpec as P

SIDE = 4
Y_LO = 2


def product_kernel(count, which_ref, offset_ref, adj_ref, *rest):
    parts, carried = rest[:count], rest[count:-2]
    out_ref, held = rest[-2:]
    block_rows, nonzero, block, _ = adj_ref.shape

    def place(part, r, k, start):
        held[r, pl.ds(k * block, block), :] = part[pl.ds(start, block), :]

    for r in range(block_rows):
        for k in range(nonzero):
            start = pl.multiple_of(offset_ref[r, k], block)
            if count == 1:
                place(parts[0], r, k, start)
            else:
                for index, part in enumerate(parts):
                    pl.when(which_ref[r, k] == index)(functools.partial(place, part, r, k, start))
    for array in carried:
        out_ref[pl.ds(block_rows * block, array.shape[0]), :] = array[...]
    for r in range(block_rows):
        left = jnp.concatenate([adj_ref[r, k] for k in range(nonzero)], axis=1)
        total = jnp.dot(left, held[r], preferred_element_type=jnp.float32)
        out_ref[pl.ds(r * block, block), :] = total.astype(out_ref.dtype)


def block_product(which, offsets, adj, parts, carried=()):
    block_rows, nonzero, block, _ = adj.shape
    width = parts[0].shape[1]
    rows = block_rows * block + sum(array.shape[0] for array in carried)
    whole = pl.BlockSpec(memory_space=pltpu.VMEM)
    return pl.pallas_call(
        functools.partial(product_kernel, len(parts)),
        out_shape=jax.ShapeDtypeStruct((rows, width), jnp.bfloat16),
        in_specs=[pl.BlockSpec(memory_space=pltpu.SMEM)] * 2 + [whole] * (1 + len(parts) + len(carried)),
        out_specs=whole,
        scratch_shapes=[pltpu.VMEM((block_rows, nonzero * block, width), jnp.bfloat16)],
        compiler_params=pltpu.CompilerParams(vmem_limit_bytes=14 << 20),
        cost_estimate=pl.CostEstimate(
            flops=2 * block_rows * nonzero * block * block * width,
            bytes_accessed=2 * (adj.size + block_rows * nonzero * block * width),
            transcendentals=0,
        ),
        name="block_product",
    )(which, offsets, adj, *parts, *carried)


def middle_kernel(here_ref, there_ref, weight_ref, parcel_ref):
    half = here_ref.shape[1]
    rows = here_ref.shape[0] // 2
    own = here_ref[:rows, :]
    logits = jnp.dot(own, weight_ref[:half, :], preferred_element_type=jnp.float32)
    logits += jnp.dot(there_ref[:rows, :], weight_ref[half:, :], preferred_element_type=jnp.float32)
    target = jnp.concatenate([here_ref[rows:, :], there_ref[rows:, :]], axis=1).astype(jnp.float32)
    logistic = jax.nn.sigmoid(logits)
    slope = logistic * (1.0 + logits * (1.0 - logistic))
    grad_out = ((logits * logistic - target) * slope).astype(jnp.bfloat16)
    back = lax.dot_general(
        grad_out, weight_ref[:half, :], (((1,), (1,)), ((), ())), preferred_element_type=jnp.float32
    ).astype(jnp.bfloat16)
    partial = lax.dot_general(own, grad_out, (((0,), (0,)), ((), ())), preferred_element_type=jnp.float32)
    head = partial.astype(jnp.bfloat16)
    rest = (partial - head.astype(jnp.float32)).astype(jnp.bfloat16)
    count = parcel_ref.shape[0]
    quarter = half // count
    width = partial.shape[1]
    for y in range(count):
        parcel_ref[y, :rows, :] = back
        start = rows
        for values in (head, rest):
            for first in range(0, width, half):
                parcel_ref[y, start : start + quarter, :] = values[y * quarter : (y + 1) * quarter, first : first + half]
                start += quarter


def middle(here, there, weight):
    rows, half = here.shape[0] // 2, here.shape[1]
    extra = 2 * weight.shape[1] // SIDE
    return pl.pallas_call(
        middle_kernel,
        out_shape=jax.ShapeDtypeStruct((SIDE, rows + extra, half), jnp.bfloat16),
        compiler_params=pltpu.CompilerParams(vmem_limit_bytes=14 << 20),
        cost_estimate=pl.CostEstimate(
            flops=4 * rows * weight.size, bytes_accessed=12 * rows * half, transcendentals=rows * weight.shape[1]
        ),
        name="middle",
    )(here, there, weight)


WHOLE = pl.BlockSpec(memory_space=pltpu.VMEM)
SMALL = pltpu.CompilerParams(vmem_limit_bytes=4 << 20)


def open_kernel(parcels_ref, quarter_ref, column_ref):
    skip = parcels_ref.shape[1] - 2 * quarter_ref.shape[0]
    half = (parcels_ref.shape[1] - skip) // 2
    pieces = parcels_ref[:, skip:, :].astype(jnp.float32)
    quarter_ref[...] = (pieces[:, :half, :] + pieces[:, half:, :]).sum(0)
    for y in range(parcels_ref.shape[0]):
        column_ref[y] = parcels_ref[y, :skip, :]


def open_parcels(parcels, skip):
    count, rows, width = parcels.shape
    return pl.pallas_call(
        open_kernel,
        out_shape=(
            jax.ShapeDtypeStruct(((rows - skip) // 2, width), jnp.float32),
            jax.ShapeDtypeStruct((count, skip, width), parcels.dtype),
        ),
        in_specs=[WHOLE],
        out_specs=(WHOLE, WHOLE),
        compiler_params=SMALL,
        name="open_parcels",
    )(parcels)


def spread_kernel(pieces_ref, *rest):
    out_ref = rest[-1]
    total = pieces_ref[...].sum(0)
    for index in range(out_ref.shape[0]):
        out_ref[index] = total


def spread_sum(pieces, count, after=()):
    return pl.pallas_call(
        spread_kernel,
        out_shape=jax.ShapeDtypeStruct((count, *pieces.shape[1:]), pieces.dtype),
        in_specs=[WHOLE] + [pl.BlockSpec(memory_space=pl.ANY)] * len(after),
        out_specs=WHOLE,
        compiler_params=SMALL,
        name="spread_sum",
    )(pieces, *after)


def settle_kernel(scale, feat_ref, pieces_ref, after_ref, out_ref):
    halves, half = out_ref.shape[1] // pieces_ref.shape[2], pieces_ref.shape[2]
    per_half = pieces_ref.shape[0] // halves
    for index in range(halves):
        values = pieces_ref[pl.ds((index ^ feat_ref[0]) * per_half, per_half)] * scale
        out_ref[:, index * half : (index + 1) * half] = values.reshape(out_ref.shape[0], half)


def settle(feat, pieces, after, scale):
    count, rows, half = pieces.shape
    return pl.pallas_call(
        functools.partial(settle_kernel, scale),
        out_shape=jax.ShapeDtypeStruct((count * rows // 2, 2 * half), pieces.dtype),
        in_specs=[pl.BlockSpec(memory_space=pltpu.SMEM), WHOLE, pl.BlockSpec(memory_space=pl.ANY)],
        out_specs=WHOLE,
        compiler_params=SMALL,
        name="settle",
    )(feat.reshape(1), pieces, after)


def to_all(value, axis, count, groups=None):
    copies = jnp.broadcast_to(value[None], (count, *value.shape))
    return lax.all_to_all(copies, axis, 0, 0, axis_index_groups=groups)


ALONG_Y = [[y * SIDE + x for y in range(SIDE)] for x in range(SIDE)]
ALONG_X = [[y * SIDE + x for x in range(SIDE)] for y in range(SIDE)]


def sum_weight(quarter, row_size):
    both = ("row", "col")
    col_size = SIDE * SIDE
    layers = row_size // Y_LO
    near = Y_LO * col_size
    mates = [
        [(z * Y_LO + lo) * col_size + y * SIDE + x for lo in range(Y_LO) for x in range(SIDE)]
        for z in range(layers)
        for y in range(SIDE)
    ]
    depth = [[z * near + i for z in range(layers)] for i in range(near)]
    plane = [[z * near + i for i in range(near)] for z in range(layers)]
    pieces = quarter.reshape(Y_LO * SIDE, -1, quarter.shape[1])
    pieces = lax.all_to_all(pieces, both, 0, 0, axis_index_groups=mates)
    pieces = lax.all_to_all(spread_sum(pieces, layers), both, 0, 0, axis_index_groups=depth)
    return lax.all_to_all(spread_sum(pieces, near), both, 0, 0, axis_index_groups=plane)


def per_device(features, adj, col_index, weight, centroid, labels):
    block_rows, nonzero, block, _ = adj.shape
    row_count, half = features.shape
    feat = lax.axis_index("feat")
    row_size, col_size = lax.axis_size("row"), lax.axis_size("col")
    node_count = row_count * row_size * col_size
    local = col_index % (block_rows * col_size)
    owner = local // block_rows
    owner_y, owner_x = owner // SIDE, owner % SIDE
    within = (local % block_rows) * block

    label_table = (
        labels[:, None] == jnp.arange(centroid.shape[0], dtype=jnp.int32)[None, :]
    ).astype(jnp.bfloat16)
    target = jnp.dot(label_table, centroid, preferred_element_type=jnp.float32).astype(jnp.bfloat16)
    swapped = jnp.roll(weight, (half, centroid.shape[1]), (0, 1))
    turned = jnp.where(feat == 0, weight, swapped)

    column = to_all(features, "col", SIDE, ALONG_Y).reshape(-1, half)
    panels = to_all(column, "col", SIDE, ALONG_X).reshape(-1, half)
    offsets = (owner_x * SIDE + owner_y) * row_count + within
    here = block_product(offsets, offsets, adj, [panels], (target,))
    there = lax.ppermute(here, "feat", [(0, 1), (1, 0)])

    parcels = lax.all_to_all(middle(here, there, turned), "col", 0, 0, axis_index_groups=ALONG_Y)
    quarter, column = open_parcels(parcels, row_count)
    column = column.reshape(-1, half)
    gathered = lax.all_gather(column, "col", axis=0, tiled=True, axis_index_groups=ALONG_X)
    feature_grad = block_product(offsets, offsets, adj, [gathered])

    weight_grad = settle(feat, sum_weight(quarter, row_size), feature_grad, 1.0 / math.sqrt(node_count))
    return (weight_grad, feature_grad)


def solution(mesh):
    placed = (
        P(("row", "col"), "feat"),
        P(("row", "col"), None, None, None),
        P(("row", "col"), None),
        P(),
        P(None, "feat"),
        P(("row", "col")),
    )
    return jax.shard_map(
        per_device,
        mesh=mesh,
        in_specs=placed,
        out_specs=(P("feat", None), P(("row", "col"), "feat")),
        check_vma=False,
    )
```

```python
import functools
import math

import jax
import jax.numpy as jnp
from jax import lax
from jax.experimental import pallas as pl
from jax.experimental.pallas import tpu as pltpu
from jax.sharding import PartitionSpec as P

SIDE = 4
WHOLE = pl.BlockSpec(memory_space=pltpu.VMEM)
SMALL = pltpu.CompilerParams(vmem_limit_bytes=4 << 20)
LARGE = 56 << 20
Y_LO = 2


def product_kernel(count, which_ref, offset_ref, adj_ref, *rest):
    parts, carried = rest[:count], rest[count:-2]
    out_ref, held = rest[-2:]
    block_rows, nonzero, block, _ = adj_ref.shape

    def place(part, r, k, start):
        held[r, pl.ds(k * block, block), :] = part[pl.ds(start, block), :]

    for r in range(block_rows):
        for k in range(nonzero):
            start = pl.multiple_of(offset_ref[r, k], block)
            if count == 1:
                place(parts[0], r, k, start)
            else:
                for index, part in enumerate(parts):
                    pl.when(which_ref[r, k] == index)(functools.partial(place, part, r, k, start))
    for array in carried:
        out_ref[pl.ds(block_rows * block, array.shape[0]), :] = array[...]
    for r in range(block_rows):
        left = jnp.concatenate([adj_ref[r, k] for k in range(nonzero)], axis=1)
        total = jnp.dot(left, held[r], preferred_element_type=jnp.float32)
        out_ref[pl.ds(r * block, block), :] = total.astype(out_ref.dtype)


def block_product(which, offsets, adj, parts, carried=()):
    block_rows, nonzero, block, _ = adj.shape
    width = parts[0].shape[1]
    rows = block_rows * block + sum(array.shape[0] for array in carried)
    whole = pl.BlockSpec(memory_space=pltpu.VMEM)
    return pl.pallas_call(
        functools.partial(product_kernel, len(parts)),
        out_shape=jax.ShapeDtypeStruct((rows, width), jnp.bfloat16),
        in_specs=[pl.BlockSpec(memory_space=pltpu.SMEM)] * 2 + [whole] * (1 + len(parts) + len(carried)),
        out_specs=whole,
        scratch_shapes=[pltpu.VMEM((block_rows, nonzero * block, width), jnp.bfloat16)],
        compiler_params=pltpu.CompilerParams(vmem_limit_bytes=14 << 20),
        cost_estimate=pl.CostEstimate(
            flops=2 * block_rows * nonzero * block * block * width,
            bytes_accessed=2 * (adj.size + block_rows * nonzero * block * width),
            transcendentals=0,
        ),
        name="block_product",
    )(which, offsets, adj, *parts, *carried)


def fetch_kernel(offset_ref, feat_ref, adj_ref, panel_ref, out_ref, same_ref, adj_held, held, adj_sems, panel_sems):
    block_rows, nonzero, block, _ = adj_held.shape
    same_ref[0] = feat_ref[0]

    def adj_copy(r):
        return pltpu.make_async_copy(adj_ref.at[r], adj_held.at[r], adj_sems.at[r])

    def panel_copy(r, k):
        start = pl.multiple_of(offset_ref[r, k], block)
        return pltpu.make_async_copy(
            panel_ref.at[pl.ds(start, block)], held.at[r, pl.ds(k * block, block)], panel_sems.at[r, k]
        )

    for r in range(block_rows):
        for k in range(nonzero):
            panel_copy(r, k).start()
        adj_copy(r).start()
    for r in range(block_rows):
        for k in range(nonzero):
            panel_copy(r, k).wait()
        adj_copy(r).wait()
        left = jnp.concatenate([adj_held[r, k] for k in range(nonzero)], axis=1)
        total = jnp.dot(left, held[r], preferred_element_type=jnp.float32)
        out_ref[pl.ds(r * block, block), :] = total.astype(out_ref.dtype)


def fetched_product(offsets, feat, adj, panels):
    block_rows, nonzero, block, _ = adj.shape
    width = panels.shape[1]
    return pl.pallas_call(
        fetch_kernel,
        out_shape=(
            jax.ShapeDtypeStruct((block_rows * block, width), jnp.bfloat16),
            jax.ShapeDtypeStruct((1,), jnp.int32),
        ),
        in_specs=[pl.BlockSpec(memory_space=pltpu.SMEM)] * 2 + [pl.BlockSpec(memory_space=pl.ANY)] * 2,
        out_specs=(WHOLE, pl.BlockSpec(memory_space=pltpu.SMEM)),
        scratch_shapes=[
            pltpu.VMEM(adj.shape, adj.dtype),
            pltpu.VMEM((block_rows, nonzero * block, width), jnp.bfloat16),
            pltpu.SemaphoreType.DMA((block_rows,)),
            pltpu.SemaphoreType.DMA((block_rows, nonzero)),
        ],
        compiler_params=pltpu.CompilerParams(vmem_limit_bytes=LARGE),
        cost_estimate=pl.CostEstimate(
            flops=2 * block_rows * nonzero * block * block * width,
            bytes_accessed=2 * (adj.size + block_rows * nonzero * block * width),
            transcendentals=0,
        ),
        name="fetched_product",
    )(offsets, feat.reshape(1), adj, panels)


def copies_kernel(value_ref, out_ref, sems):
    copies = [pltpu.make_async_copy(value_ref, out_ref.at[i], sems.at[i]) for i in range(out_ref.shape[0])]
    for copy in copies:
        copy.start()
    for copy in copies:
        copy.wait()


def copies_of(value, count):
    return pl.pallas_call(
        copies_kernel,
        out_shape=jax.ShapeDtypeStruct((count, *value.shape), value.dtype),
        in_specs=[pl.BlockSpec(memory_space=pl.ANY)],
        out_specs=pl.BlockSpec(memory_space=pl.ANY),
        scratch_shapes=[pltpu.SemaphoreType.DMA((count,))],
        compiler_params=SMALL,
        name="copies_of",
    )(value)


def middle_kernel(here_ref, there_ref, weight_ref, parcel_ref):
    half = here_ref.shape[1]
    rows = here_ref.shape[0] // 2
    own = here_ref[:rows, :]
    logits = jnp.dot(own, weight_ref[:half, :], preferred_element_type=jnp.float32)
    logits += jnp.dot(there_ref[:rows, :], weight_ref[half:, :], preferred_element_type=jnp.float32)
    target = jnp.concatenate([here_ref[rows:, :], there_ref[rows:, :]], axis=1).astype(jnp.float32)
    logistic = jax.nn.sigmoid(logits)
    slope = logistic * (1.0 + logits * (1.0 - logistic))
    grad_out = ((logits * logistic - target) * slope).astype(jnp.bfloat16)
    back = lax.dot_general(
        grad_out, weight_ref[:half, :], (((1,), (1,)), ((), ())), preferred_element_type=jnp.float32
    ).astype(jnp.bfloat16)
    partial = lax.dot_general(own, grad_out, (((0,), (0,)), ((), ())), preferred_element_type=jnp.float32)
    head = partial.astype(jnp.bfloat16)
    rest = (partial - head.astype(jnp.float32)).astype(jnp.bfloat16)
    count = parcel_ref.shape[0]
    quarter = half // count
    width = partial.shape[1]
    for y in range(count):
        parcel_ref[y, :rows, :] = back
        start = rows
        for values in (head, rest):
            for first in range(0, width, half):
                parcel_ref[y, start : start + quarter, :] = values[y * quarter : (y + 1) * quarter, first : first + half]
                start += quarter


def middle(here, there, weight):
    rows, half = here.shape[0] // 2, here.shape[1]
    extra = 2 * weight.shape[1] // SIDE
    return pl.pallas_call(
        middle_kernel,
        out_shape=jax.ShapeDtypeStruct((SIDE, rows + extra, half), jnp.bfloat16),
        compiler_params=pltpu.CompilerParams(vmem_limit_bytes=14 << 20),
        cost_estimate=pl.CostEstimate(
            flops=4 * rows * weight.size, bytes_accessed=12 * rows * half, transcendentals=rows * weight.shape[1]
        ),
        name="middle",
    )(here, there, weight)


def open_kernel(parcels_ref, quarter_ref, column_ref):
    skip = parcels_ref.shape[1] - 2 * quarter_ref.shape[0]
    half = (parcels_ref.shape[1] - skip) // 2
    pieces = parcels_ref[:, skip:, :].astype(jnp.float32)
    quarter_ref[...] = (pieces[:, :half, :] + pieces[:, half:, :]).sum(0)
    for y in range(parcels_ref.shape[0]):
        column_ref[y] = parcels_ref[y, :skip, :]


def open_parcels(parcels, skip):
    count, rows, width = parcels.shape
    return pl.pallas_call(
        open_kernel,
        out_shape=(
            jax.ShapeDtypeStruct(((rows - skip) // 2, width), jnp.float32),
            jax.ShapeDtypeStruct((count, skip, width), parcels.dtype),
        ),
        in_specs=[WHOLE],
        out_specs=(WHOLE, WHOLE),
        compiler_params=SMALL,
        name="open_parcels",
    )(parcels)


def spread_kernel(pieces_ref, *rest):
    out_ref = rest[-1]
    total = pieces_ref[...].sum(0)
    for index in range(out_ref.shape[0]):
        out_ref[index] = total


def spread_sum(pieces, count, after=()):
    return pl.pallas_call(
        spread_kernel,
        out_shape=jax.ShapeDtypeStruct((count, *pieces.shape[1:]), pieces.dtype),
        in_specs=[WHOLE] + [pl.BlockSpec(memory_space=pl.ANY)] * len(after),
        out_specs=WHOLE,
        compiler_params=SMALL,
        name="spread_sum",
    )(pieces, *after)


def settle_kernel(scale, feat_ref, pieces_ref, out_ref):
    halves, half = out_ref.shape[1] // pieces_ref.shape[2], pieces_ref.shape[2]
    per_half = pieces_ref.shape[0] // halves
    for index in range(halves):
        values = pieces_ref[pl.ds((index ^ feat_ref[0]) * per_half, per_half)] * scale
        out_ref[:, index * half : (index + 1) * half] = values.reshape(out_ref.shape[0], half)


def settle(feat, pieces, scale):
    count, rows, half = pieces.shape
    return pl.pallas_call(
        functools.partial(settle_kernel, scale),
        out_shape=jax.ShapeDtypeStruct((count * rows // 2, 2 * half), pieces.dtype),
        in_specs=[pl.BlockSpec(memory_space=pltpu.SMEM), WHOLE],
        out_specs=WHOLE,
        compiler_params=SMALL,
        name="settle",
    )(feat, pieces)


def to_all(value, axis, count, groups=None):
    copies = jnp.broadcast_to(value[None], (count, *value.shape))
    return lax.all_to_all(copies, axis, 0, 0, axis_index_groups=groups)


ALONG_Y = [[y * SIDE + x for y in range(SIDE)] for x in range(SIDE)]
ALONG_X = [[y * SIDE + x for x in range(SIDE)] for y in range(SIDE)]


def sum_weight(quarter, row_size):
    both = ("row", "col")
    col_size = SIDE * SIDE
    layers = row_size // Y_LO
    near = Y_LO * col_size
    mates = [
        [(z * Y_LO + lo) * col_size + y * SIDE + x for lo in range(Y_LO) for x in range(SIDE)]
        for z in range(layers)
        for y in range(SIDE)
    ]
    depth = [[z * near + i for z in range(layers)] for i in range(near)]
    plane = [[z * near + i for i in range(near)] for z in range(layers)]
    pieces = quarter.reshape(Y_LO * SIDE, -1, quarter.shape[1])
    pieces = lax.all_to_all(pieces, both, 0, 0, axis_index_groups=mates)
    pieces = lax.all_to_all(spread_sum(pieces, layers), both, 0, 0, axis_index_groups=depth)
    return lax.all_to_all(spread_sum(pieces, near), both, 0, 0, axis_index_groups=plane)


def per_device(features, adj, col_index, weight, centroid, labels):
    block_rows, nonzero, block, _ = adj.shape
    row_count, half = features.shape
    feat = lax.axis_index("feat")
    row_size, col_size = lax.axis_size("row"), lax.axis_size("col")
    node_count = row_count * row_size * col_size
    local = col_index % (block_rows * col_size)
    owner = local // block_rows
    owner_y, owner_x = owner // SIDE, owner % SIDE
    within = (local % block_rows) * block

    label_table = (
        labels[:, None] == jnp.arange(centroid.shape[0], dtype=jnp.int32)[None, :]
    ).astype(jnp.bfloat16)
    target = jnp.dot(label_table, centroid, preferred_element_type=jnp.float32).astype(jnp.bfloat16)
    swapped = jnp.roll(weight, (half, centroid.shape[1]), (0, 1))
    turned = jnp.where(feat == 0, weight, swapped)

    column = to_all(features, "col", SIDE, ALONG_Y).reshape(-1, half)
    panels = lax.all_to_all(copies_of(column, SIDE), "col", 0, 0, axis_index_groups=ALONG_X).reshape(-1, half)
    offsets = (owner_x * SIDE + owner_y) * row_count + within
    here = block_product(offsets, offsets, adj, [panels], (target,))
    there = lax.ppermute(here, "feat", [(0, 1), (1, 0)])

    parcels = lax.all_to_all(middle(here, there, turned), "col", 0, 0, axis_index_groups=ALONG_Y)
    quarter, column = open_parcels(parcels, row_count)
    column = column.reshape(-1, half)
    gathered = lax.all_gather(column, "col", axis=0, tiled=True, axis_index_groups=ALONG_X)
    feature_grad, same = fetched_product(offsets, feat, adj, gathered)

    weight_grad = settle(same, sum_weight(quarter, row_size), 1.0 / math.sqrt(node_count))
    return (weight_grad, feature_grad)


def solution(mesh):
    placed = (
        P(("row", "col"), "feat"),
        P(("row", "col"), None, None, None),
        P(("row", "col"), None),
        P(),
        P(None, "feat"),
        P(("row", "col")),
    )
    return jax.shard_map(
        per_device,
        mesh=mesh,
        in_specs=placed,
        out_specs=(P("feat", None), P(("row", "col"), "feat")),
        check_vma=False,
    )
```

```python
import functools
import math

import jax
import jax.numpy as jnp
from jax import lax
from jax.experimental import pallas as pl
from jax.experimental.pallas import tpu as pltpu
from jax.sharding import PartitionSpec as P

SIDE = 4
BOTH = 2
Y_LO = 2


def product_kernel(count, which_ref, offset_ref, adj_ref, *rest):
    parts, carried = rest[:count], rest[count:-2]
    out_ref, held = rest[-2:]
    block_rows, nonzero, block, _ = adj_ref.shape

    def place(part, r, k, start):
        held[r, pl.ds(k * block, block), :] = part[pl.ds(start, block), :]

    for r in range(block_rows):
        for k in range(nonzero):
            start = pl.multiple_of(offset_ref[r, k], block)
            if count == 1:
                place(parts[0], r, k, start)
            else:
                for index, part in enumerate(parts):
                    pl.when(which_ref[r, k] == index)(functools.partial(place, part, r, k, start))
    for array in carried:
        out_ref[pl.ds(block_rows * block, array.shape[0]), :] = array[...]
    for r in range(block_rows):
        left = jnp.concatenate([adj_ref[r, k] for k in range(nonzero)], axis=1)
        total = jnp.dot(left, held[r], preferred_element_type=jnp.float32)
        out_ref[pl.ds(r * block, block), :] = total.astype(out_ref.dtype)


def block_product(which, offsets, adj, parts, carried=()):
    block_rows, nonzero, block, _ = adj.shape
    width = parts[0].shape[1]
    rows = block_rows * block + sum(array.shape[0] for array in carried)
    whole = pl.BlockSpec(memory_space=pltpu.VMEM)
    return pl.pallas_call(
        functools.partial(product_kernel, len(parts)),
        out_shape=jax.ShapeDtypeStruct((rows, width), jnp.bfloat16),
        in_specs=[pl.BlockSpec(memory_space=pltpu.SMEM)] * 2 + [whole] * (1 + len(parts) + len(carried)),
        out_specs=whole,
        scratch_shapes=[pltpu.VMEM((block_rows, nonzero * block, width), jnp.bfloat16)],
        compiler_params=pltpu.CompilerParams(vmem_limit_bytes=14 << 20),
        cost_estimate=pl.CostEstimate(
            flops=2 * block_rows * nonzero * block * block * width,
            bytes_accessed=2 * (adj.size + block_rows * nonzero * block * width),
            transcendentals=0,
        ),
        name="block_product",
    )(which, offsets, adj, *parts, *carried)


def middle_kernel(here_ref, there_ref, weight_ref, partial_ref, *back_refs):
    half = here_ref.shape[1]
    rows = here_ref.shape[0] // 2
    own = here_ref[:rows, :]
    logits = jnp.dot(own, weight_ref[:half, :], preferred_element_type=jnp.float32)
    logits += jnp.dot(there_ref[:rows, :], weight_ref[half:, :], preferred_element_type=jnp.float32)
    target = jnp.concatenate([here_ref[rows:, :], there_ref[rows:, :]], axis=1).astype(jnp.float32)
    logistic = jax.nn.sigmoid(logits)
    slope = logistic * (1.0 + logits * (1.0 - logistic))
    grad_out = ((logits * logistic - target) * slope).astype(jnp.bfloat16)
    back = lax.dot_general(
        grad_out, weight_ref[:half, :], (((1,), (1,)), ((), ())), preferred_element_type=jnp.float32
    ).astype(jnp.bfloat16)
    start = 0
    for back_ref in back_refs:
        back_ref[...] = back[start : start + back_ref.shape[0], :]
        start += back_ref.shape[0]
    partial = lax.dot_general(own, grad_out, (((0,), (0,)), ((), ())), preferred_element_type=jnp.float32)
    for index in range(partial_ref.shape[0]):
        partial_ref[index] = partial[:, index * half : (index + 1) * half]


def middle(here, there, weight):
    rows, half = here.shape[0] // 2, here.shape[1]
    return pl.pallas_call(
        middle_kernel,
        out_shape=(
            jax.ShapeDtypeStruct((weight.shape[1] // half, half, half), jnp.float32),
            *[jax.ShapeDtypeStruct((rows // BOTH, half), jnp.bfloat16)] * BOTH,
        ),
        compiler_params=pltpu.CompilerParams(vmem_limit_bytes=14 << 20),
        cost_estimate=pl.CostEstimate(
            flops=4 * rows * weight.size, bytes_accessed=12 * rows * half, transcendentals=rows * weight.shape[1]
        ),
        name="middle",
    )(here, there, weight)


WHOLE = pl.BlockSpec(memory_space=pltpu.VMEM)
SMALL = pltpu.CompilerParams(vmem_limit_bytes=4 << 20)


def spread_kernel(pieces_ref, *rest):
    out_ref = rest[-1]
    total = pieces_ref[...].sum(0)
    for index in range(out_ref.shape[0]):
        out_ref[index] = total


def spread_sum(pieces, count, after=()):
    return pl.pallas_call(
        spread_kernel,
        out_shape=jax.ShapeDtypeStruct((count, *pieces.shape[1:]), pieces.dtype),
        in_specs=[WHOLE] + [pl.BlockSpec(memory_space=pl.ANY)] * len(after),
        out_specs=WHOLE,
        compiler_params=SMALL,
        name="spread_sum",
    )(pieces, *after)


def settle_kernel(scale, feat_ref, pieces_ref, out_ref):
    halves, half = out_ref.shape[1] // pieces_ref.shape[2], pieces_ref.shape[2]
    per_half = pieces_ref.shape[0] // halves
    for index in range(halves):
        values = pieces_ref[pl.ds((index ^ feat_ref[0]) * per_half, per_half)] * scale
        out_ref[:, index * half : (index + 1) * half] = values.reshape(out_ref.shape[0], half)


def settle(feat, pieces, scale):
    count, rows, half = pieces.shape
    return pl.pallas_call(
        functools.partial(settle_kernel, scale),
        out_shape=jax.ShapeDtypeStruct((count * rows // 2, 2 * half), pieces.dtype),
        in_specs=[pl.BlockSpec(memory_space=pltpu.SMEM), WHOLE],
        out_specs=WHOLE,
        compiler_params=SMALL,
        name="settle",
    )(feat.reshape(1), pieces)


def to_all(value, axis, count, groups=None):
    copies = jnp.broadcast_to(value[None], (count, *value.shape))
    return lax.all_to_all(copies, axis, 0, 0, axis_index_groups=groups)


ALONG_Y = [[y * SIDE + x for y in range(SIDE)] for x in range(SIDE)]
ALONG_X = [[y * SIDE + x for x in range(SIDE)] for y in range(SIDE)]


def sum_weight(pieces, row_size):
    both = ("row", "col")
    layers = row_size // Y_LO
    near = pieces.shape[0]
    depth = [[z * near + i for z in range(layers)] for i in range(near)]
    plane = [[z * near + i for i in range(near)] for z in range(layers)]
    pieces = lax.all_to_all(pieces, both, 0, 0, axis_index_groups=plane)
    pieces = lax.all_to_all(spread_sum(pieces, layers), both, 0, 0, axis_index_groups=depth)
    return lax.all_to_all(spread_sum(pieces, near), both, 0, 0, axis_index_groups=plane)


def per_device(features, adj, col_index, weight, centroid, labels):
    block_rows, nonzero, block, _ = adj.shape
    row_count, half = features.shape
    feat = lax.axis_index("feat")
    row_size, col_size = lax.axis_size("row"), lax.axis_size("col")
    node_count = row_count * row_size * col_size
    local = col_index % (block_rows * col_size)
    owner = local // block_rows
    owner_y, owner_x = owner // SIDE, owner % SIDE
    within = (local % block_rows) * block

    label_table = (
        labels[:, None] == jnp.arange(centroid.shape[0], dtype=jnp.int32)[None, :]
    ).astype(jnp.bfloat16)
    target = jnp.dot(label_table, centroid, preferred_element_type=jnp.float32).astype(jnp.bfloat16)
    swapped = jnp.roll(weight, (half, centroid.shape[1]), (0, 1))
    turned = jnp.where(feat == 0, weight, swapped)

    column = to_all(features, "col", SIDE, ALONG_Y).reshape(-1, half)
    panels = to_all(column, "col", SIDE, ALONG_X).reshape(-1, half)
    offsets = (owner_x * SIDE + owner_y) * row_count + within
    here = block_product(offsets, offsets, adj, [panels], (target,))
    there = lax.ppermute(here, "feat", [(0, 1), (1, 0)])

    partial, *backs = middle(here, there, turned)
    gathered = [lax.all_gather(back, "col", axis=0, tiled=True) for back in backs]
    within_rows = row_count // BOTH
    part_offsets = owner * within_rows + within % within_rows
    feature_grad = block_product(within // within_rows, part_offsets, adj, gathered)

    pieces = sum_weight(partial.reshape(Y_LO * col_size, -1, half), row_size)
    weight_grad = settle(feat, pieces, 1.0 / math.sqrt(node_count))
    return (weight_grad, feature_grad)


def solution(mesh):
    placed = (
        P(("row", "col"), "feat"),
        P(("row", "col"), None, None, None),
        P(("row", "col"), None),
        P(),
        P(None, "feat"),
        P(("row", "col")),
    )
    return jax.shard_map(
        per_device,
        mesh=mesh,
        in_specs=placed,
        out_specs=(P("feat", None), P(("row", "col"), "feat")),
        check_vma=False,
    )
```

```python
import functools
import math

import jax
import jax.numpy as jnp
from jax import lax
from jax.experimental import pallas as pl
from jax.experimental.pallas import tpu as pltpu
from jax.sharding import PartitionSpec as P

SIDE = 4
WHOLE = pl.BlockSpec(memory_space=pltpu.VMEM)
SMALL = pltpu.CompilerParams(vmem_limit_bytes=4 << 20)
Y_LO = 2


def product_kernel(offset_ref, feat_ref, adj_ref, panels_ref, out_ref, same_ref, held):
    block_rows, nonzero, block, _ = adj_ref.shape
    same_ref[0] = feat_ref[0]
    for r in range(block_rows):
        for k in range(nonzero):
            start = pl.multiple_of(offset_ref[r, k], block)
            held[r, pl.ds(k * block, block), :] = panels_ref[pl.ds(start, block), :]
    for r in range(block_rows):
        left = jnp.concatenate([adj_ref[r, k] for k in range(nonzero)], axis=1)
        total = jnp.dot(left, held[r], preferred_element_type=jnp.float32)
        out_ref[pl.ds(r * block, block), :] = total.astype(out_ref.dtype)


def block_product(offsets, feat, adj, panels):
    block_rows, nonzero, block, _ = adj.shape
    width = panels.shape[1]
    scalar = pl.BlockSpec(memory_space=pltpu.SMEM)
    return pl.pallas_call(
        product_kernel,
        out_shape=(
            jax.ShapeDtypeStruct((block_rows * block, width), jnp.bfloat16),
            jax.ShapeDtypeStruct((1,), jnp.int32),
        ),
        in_specs=[scalar, scalar, WHOLE, WHOLE],
        out_specs=(WHOLE, scalar),
        scratch_shapes=[pltpu.VMEM((block_rows, nonzero * block, width), jnp.bfloat16)],
        compiler_params=pltpu.CompilerParams(vmem_limit_bytes=14 << 20),
        cost_estimate=pl.CostEstimate(
            flops=2 * block_rows * nonzero * block * block * width,
            bytes_accessed=2 * (adj.size + block_rows * nonzero * block * width),
            transcendentals=0,
        ),
        name="block_product",
    )(offsets, feat.reshape(1), adj, panels)


def copies_kernel(value_ref, out_ref, sems):
    copies = [pltpu.make_async_copy(value_ref, out_ref.at[i], sems.at[i]) for i in range(out_ref.shape[0])]
    for copy in copies:
        copy.start()
    for copy in copies:
        copy.wait()


def copies_of(value, count):
    return pl.pallas_call(
        copies_kernel,
        out_shape=jax.ShapeDtypeStruct((count, *value.shape), value.dtype),
        in_specs=[pl.BlockSpec(memory_space=pl.ANY)],
        out_specs=pl.BlockSpec(memory_space=pl.ANY),
        scratch_shapes=[pltpu.SemaphoreType.DMA((count,))],
        compiler_params=SMALL,
        name="copies_of",
    )(value)


def middle_kernel(own_ref, other_ref, mine_ref, theirs_ref, weight_ref, parcel_ref):
    rows, half = own_ref.shape
    own = own_ref[...]
    logits = jnp.dot(own, weight_ref[:half, :], preferred_element_type=jnp.float32)
    logits += jnp.dot(other_ref[...], weight_ref[half:, :], preferred_element_type=jnp.float32)
    target = jnp.concatenate([mine_ref[...], theirs_ref[...]], axis=1).astype(jnp.float32)
    logistic = jax.nn.sigmoid(logits)
    slope = logistic * (1.0 + logits * (1.0 - logistic))
    grad_out = ((logits * logistic - target) * slope).astype(jnp.bfloat16)
    back = lax.dot_general(
        grad_out, weight_ref[:half, :], (((1,), (1,)), ((), ())), preferred_element_type=jnp.float32
    ).astype(jnp.bfloat16)
    partial = lax.dot_general(own, grad_out, (((0,), (0,)), ((), ())), preferred_element_type=jnp.float32)
    head = partial.astype(jnp.bfloat16)
    rest = (partial - head.astype(jnp.float32)).astype(jnp.bfloat16)
    count = parcel_ref.shape[0]
    quarter = half // count
    width = partial.shape[1]
    for y in range(count):
        parcel_ref[y, :rows, :] = back
        start = rows
        for values in (head, rest):
            for first in range(0, width, half):
                parcel_ref[y, start : start + quarter, :] = values[y * quarter : (y + 1) * quarter, first : first + half]
                start += quarter


def middle(own, other, mine, theirs, weight):
    rows, half = own.shape
    extra = 2 * weight.shape[1] // SIDE
    return pl.pallas_call(
        middle_kernel,
        out_shape=jax.ShapeDtypeStruct((SIDE, rows + extra, half), jnp.bfloat16),
        compiler_params=pltpu.CompilerParams(vmem_limit_bytes=14 << 20),
        cost_estimate=pl.CostEstimate(
            flops=4 * rows * weight.size, bytes_accessed=12 * rows * half, transcendentals=rows * weight.shape[1]
        ),
        name="middle",
    )(own, other, mine, theirs, weight)


def open_kernel(parcels_ref, quarter_ref, column_ref):
    skip = parcels_ref.shape[1] - 2 * quarter_ref.shape[0]
    half = (parcels_ref.shape[1] - skip) // 2
    pieces = parcels_ref[:, skip:, :].astype(jnp.float32)
    quarter_ref[...] = (pieces[:, :half, :] + pieces[:, half:, :]).sum(0)
    for y in range(parcels_ref.shape[0]):
        column_ref[y] = parcels_ref[y, :skip, :]


def open_parcels(parcels, skip):
    count, rows, width = parcels.shape
    return pl.pallas_call(
        open_kernel,
        out_shape=(
            jax.ShapeDtypeStruct(((rows - skip) // 2, width), jnp.float32),
            jax.ShapeDtypeStruct((count, skip, width), parcels.dtype),
        ),
        in_specs=[WHOLE],
        out_specs=(WHOLE, WHOLE),
        compiler_params=SMALL,
        name="open_parcels",
    )(parcels)


def spread_kernel(pieces_ref, *rest):
    out_ref = rest[-1]
    total = pieces_ref[...].sum(0)
    for index in range(out_ref.shape[0]):
        out_ref[index] = total


def spread_sum(pieces, count, after=()):
    return pl.pallas_call(
        spread_kernel,
        out_shape=jax.ShapeDtypeStruct((count, *pieces.shape[1:]), pieces.dtype),
        in_specs=[WHOLE] + [pl.BlockSpec(memory_space=pl.ANY)] * len(after),
        out_specs=WHOLE,
        compiler_params=SMALL,
        name="spread_sum",
    )(pieces, *after)


def settle_kernel(scale, feat_ref, pieces_ref, out_ref):
    halves, half = out_ref.shape[1] // pieces_ref.shape[2], pieces_ref.shape[2]
    per_half = pieces_ref.shape[0] // halves
    for index in range(halves):
        values = pieces_ref[pl.ds((index ^ feat_ref[0]) * per_half, per_half)] * scale
        out_ref[:, index * half : (index + 1) * half] = values.reshape(out_ref.shape[0], half)


def settle(feat, pieces, scale):
    count, rows, half = pieces.shape
    return pl.pallas_call(
        functools.partial(settle_kernel, scale),
        out_shape=jax.ShapeDtypeStruct((count * rows // 2, 2 * half), pieces.dtype),
        in_specs=[pl.BlockSpec(memory_space=pltpu.SMEM), WHOLE],
        out_specs=WHOLE,
        compiler_params=SMALL,
        name="settle",
    )(feat, pieces)


def to_all(value, axis, count, groups=None):
    copies = jnp.broadcast_to(value[None], (count, *value.shape))
    return lax.all_to_all(copies, axis, 0, 0, axis_index_groups=groups)


ALONG_Y = [[y * SIDE + x for y in range(SIDE)] for x in range(SIDE)]
ALONG_X = [[y * SIDE + x for x in range(SIDE)] for y in range(SIDE)]


def sum_weight(quarter, row_size):
    both = ("row", "col")
    col_size = SIDE * SIDE
    layers = row_size // Y_LO
    near = Y_LO * col_size
    mates = [
        [(z * Y_LO + lo) * col_size + y * SIDE + x for lo in range(Y_LO) for x in range(SIDE)]
        for z in range(layers)
        for y in range(SIDE)
    ]
    depth = [[z * near + i for z in range(layers)] for i in range(near)]
    plane = [[z * near + i for i in range(near)] for z in range(layers)]
    pieces = quarter.reshape(Y_LO * SIDE, -1, quarter.shape[1])
    pieces = lax.all_to_all(pieces, both, 0, 0, axis_index_groups=mates)
    pieces = lax.all_to_all(spread_sum(pieces, layers), both, 0, 0, axis_index_groups=depth)
    return lax.all_to_all(spread_sum(pieces, near), both, 0, 0, axis_index_groups=plane)


def per_device(features, adj, col_index, weight, centroid, labels):
    block_rows, nonzero, block, _ = adj.shape
    row_count, half = features.shape
    feat = lax.axis_index("feat")
    row_size, col_size = lax.axis_size("row"), lax.axis_size("col")
    node_count = row_count * row_size * col_size
    local = col_index % (block_rows * col_size)
    owner = local // block_rows
    owner_y, owner_x = owner // SIDE, owner % SIDE
    within = (local % block_rows) * block

    label_table = (
        labels[:, None] == jnp.arange(centroid.shape[0], dtype=jnp.int32)[None, :]
    ).astype(jnp.bfloat16)
    target = jnp.dot(label_table, centroid, preferred_element_type=jnp.float32).astype(jnp.bfloat16)
    theirs = lax.ppermute(target, "feat", [(0, 1), (1, 0)])
    swapped = jnp.roll(weight, (half, centroid.shape[1]), (0, 1))
    turned = jnp.where(feat == 0, weight, swapped)

    column = to_all(features, "col", SIDE, ALONG_Y).reshape(-1, half)
    panels = lax.all_to_all(copies_of(column, SIDE), "col", 0, 0, axis_index_groups=ALONG_X).reshape(-1, half)
    offsets = (owner_x * SIDE + owner_y) * row_count + within
    own, _ = block_product(offsets, feat, adj, panels)
    other = lax.ppermute(own, "feat", [(0, 1), (1, 0)])

    parcels = lax.all_to_all(middle(own, other, target, theirs, turned), "col", 0, 0, axis_index_groups=ALONG_Y)
    quarter, column = open_parcels(parcels, row_count)
    column = column.reshape(-1, half)
    gathered = lax.all_gather(column, "col", axis=0, tiled=True, axis_index_groups=ALONG_X)
    feature_grad, same = block_product(offsets, feat, adj, gathered)

    weight_grad = settle(same, sum_weight(quarter, row_size), 1.0 / math.sqrt(node_count))
    return (weight_grad, feature_grad)


def solution(mesh):
    placed = (
        P(("row", "col"), "feat"),
        P(("row", "col"), None, None, None),
        P(("row", "col"), None),
        P(),
        P(None, "feat"),
        P(("row", "col")),
    )
    return jax.shard_map(
        per_device,
        mesh=mesh,
        in_specs=placed,
        out_specs=(P("feat", None), P(("row", "col"), "feat")),
        check_vma=False,
    )
```

```python
import functools
import math

import jax
import jax.numpy as jnp
from jax import lax
from jax.experimental import pallas as pl
from jax.experimental.pallas import tpu as pltpu
from jax.sharding import PartitionSpec as P

SIDE = 4
WHOLE = pl.BlockSpec(memory_space=pltpu.VMEM)
SMALL = pltpu.CompilerParams(vmem_limit_bytes=4 << 20)
Y_LO = 2


def product_kernel(offset_ref, adj_ref, panels_ref, out_ref, last_ref, held):
    block_rows, nonzero, block, _ = adj_ref.shape
    for r in range(block_rows):
        for k in range(nonzero):
            start = pl.multiple_of(offset_ref[r, k], block)
            held[r, pl.ds(k * block, block), :] = panels_ref[pl.ds(start, block), :]
    for r in range(block_rows):
        left = jnp.concatenate([adj_ref[r, k] for k in range(nonzero)], axis=1)
        total = jnp.dot(left, held[r], preferred_element_type=jnp.float32)
        out_ref[pl.ds(r * block, block), :] = total.astype(out_ref.dtype)
    last_ref[...] = total[block - last_ref.shape[0] :, :]


def block_product(offsets, adj, panels):
    block_rows, nonzero, block, _ = adj.shape
    width = panels.shape[1]
    return pl.pallas_call(
        product_kernel,
        out_shape=(
            jax.ShapeDtypeStruct((block_rows * block, width), jnp.bfloat16),
            jax.ShapeDtypeStruct((8, width), jnp.float32),
        ),
        in_specs=[pl.BlockSpec(memory_space=pltpu.SMEM), WHOLE, WHOLE],
        out_specs=(WHOLE, WHOLE),
        scratch_shapes=[pltpu.VMEM((block_rows, nonzero * block, width), jnp.bfloat16)],
        compiler_params=pltpu.CompilerParams(vmem_limit_bytes=14 << 20),
        cost_estimate=pl.CostEstimate(
            flops=2 * block_rows * nonzero * block * block * width,
            bytes_accessed=2 * (adj.size + block_rows * nonzero * block * width),
            transcendentals=0,
        ),
        name="block_product",
    )(offsets, adj, panels)


def copies_kernel(value_ref, out_ref, sems):
    copies = [pltpu.make_async_copy(value_ref, out_ref.at[i], sems.at[i]) for i in range(out_ref.shape[0])]
    for copy in copies:
        copy.start()
    for copy in copies:
        copy.wait()


def copies_of(value, count):
    return pl.pallas_call(
        copies_kernel,
        out_shape=jax.ShapeDtypeStruct((count, *value.shape), value.dtype),
        in_specs=[pl.BlockSpec(memory_space=pl.ANY)],
        out_specs=pl.BlockSpec(memory_space=pl.ANY),
        scratch_shapes=[pltpu.SemaphoreType.DMA((count,))],
        compiler_params=SMALL,
        name="copies_of",
    )(value)


def middle_kernel(own_ref, other_ref, mine_ref, theirs_ref, weight_ref, parcel_ref):
    rows, half = own_ref.shape
    own = own_ref[...]
    logits = jnp.dot(own, weight_ref[:half, :], preferred_element_type=jnp.float32)
    logits += jnp.dot(other_ref[...], weight_ref[half:, :], preferred_element_type=jnp.float32)
    target = jnp.concatenate([mine_ref[...], theirs_ref[...]], axis=1).astype(jnp.float32)
    logistic = jax.nn.sigmoid(logits)
    slope = logistic * (1.0 + logits * (1.0 - logistic))
    grad_out = ((logits * logistic - target) * slope).astype(jnp.bfloat16)
    back = lax.dot_general(
        grad_out, weight_ref[:half, :], (((1,), (1,)), ((), ())), preferred_element_type=jnp.float32
    ).astype(jnp.bfloat16)
    partial = lax.dot_general(own, grad_out, (((0,), (0,)), ((), ())), preferred_element_type=jnp.float32)
    head = partial.astype(jnp.bfloat16)
    rest = (partial - head.astype(jnp.float32)).astype(jnp.bfloat16)
    count = parcel_ref.shape[0]
    quarter = half // count
    width = partial.shape[1]
    for y in range(count):
        parcel_ref[y, :rows, :] = back
        start = rows
        for values in (head, rest):
            for first in range(0, width, half):
                parcel_ref[y, start : start + quarter, :] = values[y * quarter : (y + 1) * quarter, first : first + half]
                start += quarter


def middle(own, other, mine, theirs, weight):
    rows, half = own.shape
    extra = 2 * weight.shape[1] // SIDE
    return pl.pallas_call(
        middle_kernel,
        out_shape=jax.ShapeDtypeStruct((SIDE, rows + extra, half), jnp.bfloat16),
        compiler_params=pltpu.CompilerParams(vmem_limit_bytes=14 << 20),
        cost_estimate=pl.CostEstimate(
            flops=4 * rows * weight.size, bytes_accessed=12 * rows * half, transcendentals=rows * weight.shape[1]
        ),
        name="middle",
    )(own, other, mine, theirs, weight)


def open_kernel(parcels_ref, quarter_ref, column_ref):
    skip = parcels_ref.shape[1] - 2 * quarter_ref.shape[0]
    half = (parcels_ref.shape[1] - skip) // 2
    pieces = parcels_ref[:, skip:, :].astype(jnp.float32)
    quarter_ref[...] = (pieces[:, :half, :] + pieces[:, half:, :]).sum(0)
    for y in range(parcels_ref.shape[0]):
        column_ref[y] = parcels_ref[y, :skip, :]


def open_parcels(parcels, skip):
    count, rows, width = parcels.shape
    return pl.pallas_call(
        open_kernel,
        out_shape=(
            jax.ShapeDtypeStruct(((rows - skip) // 2, width), jnp.float32),
            jax.ShapeDtypeStruct((count, skip, width), parcels.dtype),
        ),
        in_specs=[WHOLE],
        out_specs=(WHOLE, WHOLE),
        compiler_params=SMALL,
        name="open_parcels",
    )(parcels)


def spread_kernel(pieces_ref, *rest):
    out_ref = rest[-1]
    total = pieces_ref[...].sum(0)
    for index in range(out_ref.shape[0]):
        out_ref[index] = total


def spread_sum(pieces, count, after=()):
    return pl.pallas_call(
        spread_kernel,
        out_shape=jax.ShapeDtypeStruct((count, *pieces.shape[1:]), pieces.dtype),
        in_specs=[WHOLE] + [pl.BlockSpec(memory_space=pl.ANY)] * len(after),
        out_specs=WHOLE,
        compiler_params=SMALL,
        name="spread_sum",
    )(pieces, *after)


def settle_kernel(scale, feat_ref, pieces_ref, last_ref, out_ref):
    halves, half = out_ref.shape[1] // pieces_ref.shape[2], pieces_ref.shape[2]
    per_half = pieces_ref.shape[0] // halves
    for index in range(halves):
        values = pieces_ref[pl.ds((index ^ feat_ref[0]) * per_half, per_half)] * scale
        out_ref[:, index * half : (index + 1) * half] = values.reshape(out_ref.shape[0], half)


def settle(feat, pieces, last, scale):
    count, rows, half = pieces.shape
    return pl.pallas_call(
        functools.partial(settle_kernel, scale),
        out_shape=jax.ShapeDtypeStruct((count * rows // 2, 2 * half), pieces.dtype),
        in_specs=[pl.BlockSpec(memory_space=pltpu.SMEM), WHOLE, WHOLE],
        out_specs=WHOLE,
        compiler_params=SMALL,
        name="settle",
    )(feat.reshape(1), pieces, last)


def to_all(value, axis, count, groups=None):
    copies = jnp.broadcast_to(value[None], (count, *value.shape))
    return lax.all_to_all(copies, axis, 0, 0, axis_index_groups=groups)


ALONG_Y = [[y * SIDE + x for y in range(SIDE)] for x in range(SIDE)]
ALONG_X = [[y * SIDE + x for x in range(SIDE)] for y in range(SIDE)]


def sum_weight(quarter, row_size):
    both = ("row", "col")
    col_size = SIDE * SIDE
    layers = row_size // Y_LO
    near = Y_LO * col_size
    mates = [
        [(z * Y_LO + lo) * col_size + y * SIDE + x for lo in range(Y_LO) for x in range(SIDE)]
        for z in range(layers)
        for y in range(SIDE)
    ]
    depth = [[z * near + i for z in range(layers)] for i in range(near)]
    plane = [[z * near + i for i in range(near)] for z in range(layers)]
    pieces = quarter.reshape(Y_LO * SIDE, -1, quarter.shape[1])
    pieces = lax.all_to_all(pieces, both, 0, 0, axis_index_groups=mates)
    pieces = lax.all_to_all(spread_sum(pieces, layers), both, 0, 0, axis_index_groups=depth)
    return lax.all_to_all(spread_sum(pieces, near), both, 0, 0, axis_index_groups=plane)


def per_device(features, adj, col_index, weight, centroid, labels):
    block_rows, nonzero, block, _ = adj.shape
    row_count, half = features.shape
    feat = lax.axis_index("feat")
    row_size, col_size = lax.axis_size("row"), lax.axis_size("col")
    node_count = row_count * row_size * col_size
    local = col_index % (block_rows * col_size)
    owner = local // block_rows
    owner_y, owner_x = owner // SIDE, owner % SIDE
    within = (local % block_rows) * block

    label_table = (
        labels[:, None] == jnp.arange(centroid.shape[0], dtype=jnp.int32)[None, :]
    ).astype(jnp.bfloat16)
    target = jnp.dot(label_table, centroid, preferred_element_type=jnp.float32).astype(jnp.bfloat16)
    theirs = lax.ppermute(target, "feat", [(0, 1), (1, 0)])
    swapped = jnp.roll(weight, (half, centroid.shape[1]), (0, 1))
    turned = jnp.where(feat == 0, weight, swapped)

    column = to_all(features, "col", SIDE, ALONG_Y).reshape(-1, half)
    panels = lax.all_to_all(copies_of(column, SIDE), "col", 0, 0, axis_index_groups=ALONG_X).reshape(-1, half)
    offsets = (owner_x * SIDE + owner_y) * row_count + within
    own, _ = block_product(offsets, adj, panels)
    other = lax.ppermute(own, "feat", [(0, 1), (1, 0)])

    parcels = lax.all_to_all(middle(own, other, target, theirs, turned), "col", 0, 0, axis_index_groups=ALONG_Y)
    quarter, column = open_parcels(parcels, row_count)
    column = column.reshape(-1, half)
    gathered = lax.all_gather(column, "col", axis=0, tiled=True, axis_index_groups=ALONG_X)
    feature_grad, last = block_product(offsets, adj, gathered)

    weight_grad = settle(feat, sum_weight(quarter, row_size), last, 1.0 / math.sqrt(node_count))
    return (weight_grad, feature_grad)


def solution(mesh):
    placed = (
        P(("row", "col"), "feat"),
        P(("row", "col"), None, None, None),
        P(("row", "col"), None),
        P(),
        P(None, "feat"),
        P(("row", "col")),
    )
    return jax.shard_map(
        per_device,
        mesh=mesh,
        in_specs=placed,
        out_specs=(P("feat", None), P(("row", "col"), "feat")),
        check_vma=False,
    )
```
